128 devices in a mesh: row: 8 (over x, y_hi), col: 16 (over z, y_lo, core).
Axes of the slice: x: 4, y: 4 (y_hi: 2, y_lo: 2; y = y_hi * 2 + y_lo), z: 4, core: 2. Of those that a mesh axis runs over, the one named last changes fastest.
Arguments:
- vectors: bfloat16 [131072, 128], P(('row', 'col')), may hold values from -6 to 6
- tiles: bfloat16 [20480, 256, 256], P(('row', 'col')), may hold values from -0.03125 to 0.03125
- tile_rows: int32 [20480], P(('row', 'col')), may hold values from 0 to 63
- tile_cols: int32 [20480], P(('row', 'col')), may hold values from 0 to 31
- tile_count: int32 [128], P(('row', 'col')), may hold values from 40 to 160, as said below
Outputs:
- filtered: float32 [131072, 128], P(('row', 'col'))
The draws below stay inside these ranges and needn't reach their ends.
Inputs may be any that keep to these rules, and one draw needn't show every extreme that they name: `tile_count`: slots of a device at and beyond its count are empty: their tiles and indices carry no meaning; exactly one device has 160 live slots.
All inputs are finite; a program needn't handle non-finite values.
Results may differ from the reference program's by a relative error of at most 0.015.
Values may be sent and summed in bfloat16 or wider, within the bound.
No kernel may reach another device: no remote copies, remote signals or barrier semaphores. Data moves between devices by JAX's collectives and lax.ppermute only.
A program may use at most 192 MiB of HBM per device.

```python
import jax
import jax.numpy as jnp
from jax import lax

BS = 256
NV = 128
ROWS_DEV = 4
TILE_DEV = 160
GRID = 128
NBLK = 512
ORDER = 131072
SLOTS = 20480
N_ROW = 8
N_COL = 16


def draw_tile_count(key, part):
    key = jax.random.fold_in(key, 11)
    base_key, full_key = jax.random.split(key)
    counts = TILE_DEV // 4 + jax.random.randint(base_key, (GRID,), 0, TILE_DEV // 2 + 1)
    busiest = jax.random.randint(full_key, (), 0, GRID)
    return jnp.where(jnp.arange(GRID) == busiest, TILE_DEV, counts).astype(jnp.int32)


def place_ends(array, stream_key, low, high):
    spot = [jax.random.randint(jax.random.fold_in(stream_key, axis), (), 0, length) for axis, length in enumerate(array.shape)]
    main_axis = array.shape.index(max(array.shape))
    neighbour = spot[:main_axis] + [(spot[main_axis] + 1) % array.shape[main_axis]] + spot[main_axis + 1:]
    return array.at[tuple(spot)].set(low).at[tuple(neighbour)].set(high)


def level_of(own_key, dims, shards, low, high):
    gain, own = 1.0, jax.random.fold_in(own_key, 6)
    for axis_at, blocks in shards:
        heights = jnp.exp(jax.random.uniform(jax.random.fold_in(own, axis_at), (blocks,), jnp.float32, low / len(shards), high / len(shards)))
        gain = gain * jnp.repeat(heights, dims[axis_at] // blocks).reshape([-1 if axis == axis_at else 1 for axis in range(len(dims))])
    return gain


def gaussian(own_key, extent, spread, bound, cuts=(), kind=jnp.bfloat16):
    drawn = spread * jax.random.normal(own_key, extent, jnp.float32)
    if cuts:
        drawn = drawn * level_of(own_key, extent, cuts, -0.22, 0.18)
    return jnp.clip(drawn, -bound, bound).astype(kind)


def setup_inputs(seed: int = 0) -> dict:
    streams_of = jax.random.split(jax.random.key(seed), 6)
    return {
        "vectors": gaussian(streams_of[0], (ORDER, NV), 1.0, 6.0, ((0, 128),)),
        "tiles": gaussian(streams_of[1], (SLOTS, BS, BS), (4 * BS * TILE_DEV // ROWS_DEV) ** -0.5, 0.03125, ((0, 128),)),
        "tile_rows": place_ends(jax.random.randint(streams_of[2], (SLOTS,), 0, N_COL * ROWS_DEV), jax.random.fold_in(streams_of[2], 1), 0, (N_COL * ROWS_DEV) - 1).astype(jnp.int32),
        "tile_cols": place_ends(jax.random.randint(streams_of[3], (SLOTS,), 0, N_ROW * ROWS_DEV), jax.random.fold_in(streams_of[3], 1), 0, (N_ROW * ROWS_DEV) - 1).astype(jnp.int32),
        "tile_count": draw_tile_count(jax.random.fold_in(streams_of[5], 71), 0),
    }


center_value = 0.5
radius_value = 1.5


def apply_matrix(field, tile_grid, rows_glob, cols_glob, cols_local, live_mask):
    device_ids = jnp.arange(N_ROW * N_COL, dtype=jnp.int32)

    def add_device(running, items):
        tile_set, row_index, col_index, col_local, mask, device = items
        grid_row = device // N_COL
        grid_col = device % N_COL
        tile_float = tile_set.astype(jnp.float32)
        direct = jnp.einsum("tab,tbk->tak", tile_float, field[col_index].astype(jnp.float32), precision=lax.Precision.HIGHEST)
        direct = direct * mask[:, None, None]
        mirror = jnp.einsum("tba,tbk->tak", tile_float, field[row_index].astype(jnp.float32), precision=lax.Precision.HIGHEST)
        mirror = mirror * mask[:, None, None]
        row_start = (grid_row * (N_COL * ROWS_DEV)).astype(jnp.int32)
        direct_part = jnp.zeros((N_COL * ROWS_DEV, BS, NV), jnp.float32).at[row_index - row_start].add(direct)
        direct_part = lax.optimization_barrier(direct_part.astype(jnp.bfloat16)).astype(jnp.float32)
        current = lax.dynamic_slice_in_dim(running, row_start, N_COL * ROWS_DEV, 0)
        running = lax.dynamic_update_slice_in_dim(running, current + direct_part, row_start, 0)
        mirror_part = jnp.zeros((N_ROW * ROWS_DEV, BS, NV), jnp.float32).at[col_local].add(mirror)
        mirror_part = lax.optimization_barrier(mirror_part.astype(jnp.bfloat16)).astype(jnp.float32)
        local_ids = jnp.arange(N_ROW * ROWS_DEV, dtype=jnp.int32)
        col_set = ((local_ids // ROWS_DEV) * N_COL + grid_col) * ROWS_DEV + local_ids % ROWS_DEV
        running = running.at[col_set].add(mirror_part)
        return running, None

    start_sum = jnp.zeros((NBLK, BS, NV), jnp.float32)
    running, _ = lax.scan(add_device, start_sum, (tile_grid, rows_glob, cols_glob, cols_local, live_mask, device_ids))
    return running


def reference(vectors, tiles, tile_rows, tile_cols, tile_count):
    grid_devices = N_ROW * N_COL
    device_ids = jnp.arange(grid_devices, dtype=jnp.int32)
    rows_local = tile_rows.reshape(grid_devices, TILE_DEV)
    cols_local = tile_cols.reshape(grid_devices, TILE_DEV)
    rows_glob = (device_ids // N_COL)[:, None] * (N_COL * ROWS_DEV) + rows_local
    cols_glob = ((cols_local // ROWS_DEV) * N_COL + (device_ids % N_COL)[:, None]) * ROWS_DEV + cols_local % ROWS_DEV
    live_mask = (jnp.arange(TILE_DEV, dtype=jnp.int32)[None, :] < tile_count[:, None]).astype(jnp.float32)
    tile_grid = tiles.reshape(grid_devices, TILE_DEV, BS, BS)
    x_float = vectors.astype(jnp.float32)
    applied = apply_matrix(vectors.reshape(NBLK, BS, NV), tile_grid, rows_glob, cols_glob, cols_local, live_mask)
    applied = applied.reshape(ORDER, NV)
    first_term = ((applied - center_value * x_float) / radius_value).astype(jnp.bfloat16)
    second = apply_matrix(first_term.reshape(NBLK, BS, NV), tile_grid, rows_glob, cols_glob, cols_local, live_mask)
    second = second.reshape(ORDER, NV)
    return 2.0 * (second - center_value * first_term.astype(jnp.float32)) / radius_value - x_float
```

```python
import functools

import jax
import jax.numpy as jnp
from jax import lax
from jax.experimental import pallas as pl
from jax.experimental.pallas import tpu as pltpu
from jax.sharding import PartitionSpec as P

center_value = 0.5
radius_value = 1.5

BS = 256
NV = 128
OWN = 4
CHUNK = 16

ROW_STEPS = [(dx, dy) for dx in range(4) for dy in range(2)]
COL_STEPS = [(dz, dy) for dz in range(4) for dy in range(2)]


def send_row(value, step):
    dx, dy = step
    pairs = [(x * 2 + y, (x + dx) % 4 * 2 + (y ^ dy)) for x in range(4) for y in range(2)]
    return lax.ppermute(value, "row", pairs)


def send_col(value, step, dk=0):
    dz, dy = step
    pairs = [
        (z * 4 + y * 2 + k, (z + dz) % 4 * 4 + (y ^ dy) * 2 + (k ^ dk))
        for z in range(4)
        for y in range(2)
        for k in range(2)
    ]
    return lax.ppermute(value, "col", pairs)


def spmv_kernel(mirror, n_in, n_out, out_slot, in_slot, count, tiles, *rest):
    v_in = rest[:n_in]
    outs = rest[n_in : n_in + n_out]
    acc, held, sems = rest[n_in + n_out :]
    step = pl.program_id(0)

    @pl.when(step == 0)
    def _():
        part = held.shape[0] // n_in
        copies = [
            pltpu.make_async_copy(v_in[j], held.at[pl.ds(j * part, part)], sems.at[j])
            for j in range(n_in)
        ]
        for copy in copies:
            copy.start()
        acc[...] = jnp.zeros_like(acc)
        for copy in copies:
            copy.wait()

    @pl.when(step * CHUNK < count[0])
    def _():
        for j in range(CHUNK):
            slot = step * CHUNK + j
            base = pl.multiple_of(in_slot[slot] * BS, BS)
            vec = held[pl.ds(base, BS), :]
            dims = (((0,), (0,)), ((), ())) if mirror else (((1,), (0,)), ((), ()))
            acc[out_slot[slot]] += lax.dot_general(
                tiles[j], vec, dims, preferred_element_type=jnp.float32
            )

    @pl.when(step == pl.num_programs(0) - 1)
    def _():
        at = 0
        for out in outs:
            blocks = out.shape[0] // BS

            @pl.loop(0, blocks)
            def _(b):
                out[pl.ds(pl.multiple_of(b * BS, BS), BS), :] = acc[at + b].astype(out.dtype)

            at += blocks


def spmv(mirror, tiles, out_slot, in_slot, count, v_in, out_rows):
    slots = tiles.shape[0]
    n_in, n_out = len(v_in), len(out_rows)
    blocks_out = sum(out_rows) // BS

    def tile_index(i, out_slot, in_slot, count):
        last = jnp.maximum((count[0] + CHUNK - 1) // CHUNK - 1, 0)
        return jnp.minimum(i, last), 0, 0

    return pl.pallas_call(
        functools.partial(spmv_kernel, mirror, n_in, n_out),
        grid_spec=pltpu.PrefetchScalarGridSpec(
            num_scalar_prefetch=3,
            grid=(slots // CHUNK,),
            in_specs=[pl.BlockSpec((CHUNK, BS, BS), tile_index)]
            + [pl.BlockSpec(memory_space=pl.ANY)] * n_in,
            out_specs=[pl.BlockSpec((n, NV), lambda i, *_: (0, 0)) for n in out_rows],
            scratch_shapes=[
                pltpu.VMEM((blocks_out + 1, BS, NV), jnp.float32),
                pltpu.VMEM((sum(v.shape[0] for v in v_in), NV), jnp.bfloat16),
                pltpu.SemaphoreType.DMA((n_in,)),
            ],
        ),
        out_shape=[jax.ShapeDtypeStruct((n, NV), jnp.bfloat16) for n in out_rows],
        compiler_params=pltpu.CompilerParams(vmem_limit_bytes=56 * 2**20),
        cost_estimate=pl.CostEstimate(
            flops=2 * slots * BS * BS * NV, bytes_accessed=slots * BS * BS * 2, transcendentals=0
        ),
        name="mirror_sums" if mirror else "direct_sums",
    )(out_slot, in_slot, count, tiles, *v_in)


def gather_row(field):
    parts = {(0, 0): field, (0, 1): send_row(field, (0, 1))}
    for dx in (2, 1, 3):
        parts[dx, 0] = send_row(field, (dx, 0))
    for dx in (2, 1, 3):
        parts[dx, 1] = send_row(parts[0, 1], (dx, 0))
    return [parts[step] for step in ROW_STEPS]


def gather_col(field):
    return [lax.all_gather(field, "col", axis=0, tiled=True)]


def scatter_col(chunks):
    groups = [[at * 2 + k for at in range(8)] for k in range(2)]
    return lax.all_to_all(chunks, "col", 0, 0, axis_index_groups=groups, tiled=True)


def apply(field, tiles, slots, count):
    direct_out, direct_in, mirror_out, mirror_in = slots
    rows = OWN * BS
    row_parts = gather_row(field)
    col_parts = gather_col(field)
    mine, other = spmv(False, tiles, direct_out, direct_in, count, row_parts, [8 * rows, 8 * rows])
    theirs = send_col(other, (0, 0), 1)
    mirrored = spmv(True, tiles, mirror_out, mirror_in, count, col_parts, [rows] * 8)
    chunks = (mine.astype(jnp.float32) + theirs.astype(jnp.float32)).astype(jnp.bfloat16)
    parts = list(scatter_col(chunks).reshape(8, rows, NV))
    parts += [c if step == (0, 0) else send_row(c, step) for step, c in zip(ROW_STEPS, mirrored)]
    return sum(part.astype(jnp.float32) for part in parts)


def local(vectors, tiles, tile_rows, tile_cols, tile_count):
    row_at = lax.axis_index("row")
    col_at = lax.axis_index("col")
    x, yh = row_at // 2, row_at % 2
    k = col_at % 2
    live = jnp.arange(tiles.shape[0], dtype=jnp.int32) < tile_count[0]
    own_r = tile_rows // OWN
    oz, oy, ok = own_r // 4, own_r // 2 % 2, own_r % 2
    to_col = (oz * 2 + oy + (ok ^ k) * 8) * OWN + tile_rows % OWN
    from_col = tile_rows
    own_c = tile_cols // OWN
    ox, oh = own_c // 2, own_c % 2
    to_row = ((ox - x) % 4 * 2 + (oh ^ yh)) * OWN + tile_cols % OWN
    from_row = ((x - ox) % 4 * 2 + (oh ^ yh)) * OWN + tile_cols % OWN
    slots = (
        jnp.where(live, to_col, 16 * OWN),
        jnp.where(live, from_row, 0),
        jnp.where(live, to_row, 8 * OWN),
        jnp.where(live, from_col, 0),
    )
    x_float = vectors.astype(jnp.float32)
    applied = apply(vectors, tiles, slots, tile_count)
    first_term = ((applied - center_value * x_float) / radius_value).astype(jnp.bfloat16)
    second = apply(first_term, tiles, slots, tile_count)
    return 2.0 * (second - center_value * first_term.astype(jnp.float32)) / radius_value - x_float


def solution(mesh):
    return jax.shard_map(
        local,
        mesh=mesh,
        in_specs=(
            P(("row", "col"), None),
            P(("row", "col"), None, None),
            P(("row", "col")),
            P(("row", "col")),
            P(("row", "col")),
        ),
        out_specs=P(("row", "col"), None),
        check_vma=False,
    )
```

```python
import functools

import jax
import jax.numpy as jnp
from jax import lax
from jax.experimental import pallas as pl
from jax.experimental.pallas import tpu as pltpu
from jax.sharding import PartitionSpec as P

center_value = 0.5
radius_value = 1.5

BS = 256
NV = 128
OWN = 4
CHUNK = 16
RING = 3
LIMIT = {False: 48, True: 60}

ROW_STEPS = [(dx, dy) for dx in range(4) for dy in range(2)]
COL_STEPS = [(dz, dy) for dz in range(4) for dy in range(2)]


def send_row(value, step):
    dx, dy = step
    pairs = [(x * 2 + y, (x + dx) % 4 * 2 + (y ^ dy)) for x in range(4) for y in range(2)]
    return lax.ppermute(value, "row", pairs)


def send_col(value, step, dk=0):
    dz, dy = step
    pairs = [
        (z * 4 + y * 2 + k, (z + dz) % 4 * 4 + (y ^ dy) * 2 + (k ^ dk))
        for z in range(4)
        for y in range(2)
        for k in range(2)
    ]
    return lax.ppermute(value, "col", pairs)


def spmv_kernel(mirror, n_in, n_out, out_slot, in_slot, count, tiles, *rest):
    v_in = rest[:n_in]
    outs = rest[n_in : n_in + n_out]
    acc, held, ring, in_sems, ring_sems = rest[n_in + n_out :]
    depth = ring.shape[0]
    steps = (count[0] + CHUNK - 1) // CHUNK

    def fetch(step):
        at = lax.rem(step, depth)
        return pltpu.make_async_copy(
            tiles.at[pl.ds(step * CHUNK, CHUNK)], ring.at[at], ring_sems.at[at]
        )

    part = held.shape[0] // n_in
    copies = [
        pltpu.make_async_copy(v_in[j], held.at[pl.ds(j * part, part)], in_sems.at[j])
        for j in range(n_in)
    ]
    for copy in copies:
        copy.start()
    for step in range(depth - 1):

        @pl.when(step < steps)
        def _():
            fetch(step).start()

    acc[...] = jnp.zeros_like(acc)
    for copy in copies:
        copy.wait()

    @pl.loop(0, steps)
    def _(step):
        @pl.when(step + depth - 1 < steps)
        def _():
            fetch(step + depth - 1).start()

        fetch(step).wait()
        at = lax.rem(step, depth)
        for j in range(CHUNK):
            slot = step * CHUNK + j
            base = pl.multiple_of(in_slot[slot] * BS, BS)
            vec = held[pl.ds(base, BS), :]
            dims = (((0,), (0,)), ((), ())) if mirror else (((1,), (0,)), ((), ()))
            acc[out_slot[slot]] += lax.dot_general(
                ring[at, j], vec, dims, preferred_element_type=jnp.float32
            )

    at = 0
    for out in outs:
        for b in range(out.shape[0] // BS):
            out[b * BS : (b + 1) * BS, :] = acc[at].astype(out.dtype)
            at += 1


def spmv(mirror, tiles, out_slot, in_slot, count, v_in, out_rows):
    slots = tiles.shape[0]
    n_in, n_out = len(v_in), len(out_rows)
    blocks_out = sum(out_rows) // BS
    return pl.pallas_call(
        functools.partial(spmv_kernel, mirror, n_in, n_out),
        in_specs=[pl.BlockSpec(memory_space=pltpu.SMEM)] * 3
        + [pl.BlockSpec(memory_space=pl.ANY)] * (1 + n_in),
        out_specs=[pl.BlockSpec(memory_space=pltpu.VMEM)] * n_out,
        scratch_shapes=[
            pltpu.VMEM((blocks_out + 1, BS, NV), jnp.float32),
            pltpu.VMEM((sum(v.shape[0] for v in v_in), NV), jnp.bfloat16),
            pltpu.VMEM((RING, CHUNK, BS, BS), jnp.bfloat16),
            pltpu.SemaphoreType.DMA((n_in,)),
            pltpu.SemaphoreType.DMA((RING,)),
        ],
        out_shape=[jax.ShapeDtypeStruct((n, NV), jnp.bfloat16) for n in out_rows],
        compiler_params=pltpu.CompilerParams(vmem_limit_bytes=LIMIT[mirror] * 2**20),
        cost_estimate=pl.CostEstimate(
            flops=2 * slots * BS * BS * NV, bytes_accessed=slots * BS * BS * 2, transcendentals=0
        ),
        name="mirror_sums" if mirror else "direct_sums",
    )(out_slot, in_slot, count, tiles, *v_in)


def gather_row(field):
    parts = {(0, 0): field, (0, 1): send_row(field, (0, 1))}
    for dx in (2, 1, 3):
        parts[dx, 0] = send_row(field, (dx, 0))
    for dx in (1, 3):
        parts[dx, 1] = send_row(parts[0, 1], (dx, 0))
    parts[2, 1] = send_row(parts[2, 0], (0, 1))
    return [parts[step] for step in ROW_STEPS]


def gather_col(field):
    return [lax.all_gather(field, "col", axis=0, tiled=True)]


def total(parts):
    return sum(part.astype(jnp.float32) for part in parts)


def rounded(parts):
    return parts[0] if len(parts) == 1 else total(parts).astype(jnp.bfloat16)


def scatter(send, own, beside, up, far, far_beside, down):
    rows = own[0].shape[0]
    passed = send(rounded(far_beside), (0, 1))
    up, down = send(rounded(up), (1, 0)), send(rounded(down), (3, 0))
    far = send(rounded(far + [passed]), (2, 0))
    beside = send(rounded(beside + [up[rows:], down[rows:]]), (0, 1))
    return own + [up[:rows], down[:rows], far, beside]


def apply(field, tiles, slots, count):
    direct_out, direct_in, mirror_out, mirror_in = slots
    rows = OWN * BS
    split = [rows, rows, 2 * rows, rows, rows, 2 * rows]
    row_parts = gather_row(field)
    col_parts = gather_col(field)
    *mine, other = spmv(False, tiles, direct_out, direct_in, count, row_parts, split + [8 * rows])
    theirs = jnp.split(send_col(other, (0, 0), 1), [rows, 2 * rows, 4 * rows, 5 * rows, 6 * rows])
    mirrored = spmv(True, tiles, mirror_out, mirror_in, count, col_parts, split)
    parts = scatter(send_col, *([a, b] for a, b in zip(mine, theirs)))
    parts += scatter(send_row, *([a] for a in mirrored))
    return total(parts)


def local(vectors, tiles, tile_rows, tile_cols, tile_count):
    row_at = lax.axis_index("row")
    col_at = lax.axis_index("col")
    x, yh = row_at // 2, row_at % 2
    z, yl, k = col_at // 4, col_at // 2 % 2, col_at % 2
    live = jnp.arange(tiles.shape[0], dtype=jnp.int32) < tile_count[0]
    own_r = tile_rows // OWN
    oz, oy, ok = own_r // 4, own_r // 2 % 2, own_r % 2
    to_col = ((oz - z) % 4 * 2 + (oy ^ yl) + (ok ^ k) * 8) * OWN + tile_rows % OWN
    from_col = tile_rows
    own_c = tile_cols // OWN
    ox, oh = own_c // 2, own_c % 2
    to_row = ((ox - x) % 4 * 2 + (oh ^ yh)) * OWN + tile_cols % OWN
    from_row = ((x - ox) % 4 * 2 + (oh ^ yh)) * OWN + tile_cols % OWN
    slots = (
        jnp.where(live, to_col, 16 * OWN),
        jnp.where(live, from_row, 0),
        jnp.where(live, to_row, 8 * OWN),
        jnp.where(live, from_col, 0),
    )
    x_float = vectors.astype(jnp.float32)
    applied = apply(vectors, tiles, slots, tile_count)
    first_term = ((applied - center_value * x_float) / radius_value).astype(jnp.bfloat16)
    second = apply(first_term, tiles, slots, tile_count)
    return 2.0 * (second - center_value * first_term.astype(jnp.float32)) / radius_value - x_float


def solution(mesh):
    return jax.shard_map(
        local,
        mesh=mesh,
        in_specs=(
            P(("row", "col"), None),
            P(("row", "col"), None, None),
            P(("row", "col")),
            P(("row", "col")),
            P(("row", "col")),
        ),
        out_specs=P(("row", "col"), None),
        check_vma=False,
    )
```

```python
import functools

import jax
import jax.numpy as jnp
from jax import lax
from jax.experimental import pallas as pl
from jax.experimental.pallas import tpu as pltpu
from jax.sharding import PartitionSpec as P

center_value = 0.5
radius_value = 1.5

BS = 256
NV = 128
OWN = 4
CHUNK = 16
RING = 3
LIMIT = {False: 48, True: 60}

ROW_STEPS = [(dx, dy) for dx in range(4) for dy in range(2)]
COL_STEPS = [(dz, dy) for dz in range(4) for dy in range(2)]


def send_row(value, step):
    dx, dy = step
    pairs = [(x * 2 + y, (x + dx) % 4 * 2 + (y ^ dy)) for x in range(4) for y in range(2)]
    return lax.ppermute(value, "row", pairs)


def send_col(value, step, dk=0):
    dz, dy = step
    pairs = [
        (z * 4 + y * 2 + k, (z + dz) % 4 * 4 + (y ^ dy) * 2 + (k ^ dk))
        for z in range(4)
        for y in range(2)
        for k in range(2)
    ]
    return lax.ppermute(value, "col", pairs)


def spmv_kernel(mirror, n_in, n_out, order, out_slot, in_slot, begin, stop, tiles, *rest):
    v_in = rest[:n_in]
    outs = rest[n_in : n_in + n_out]
    acc, held, ring, in_sems, ring_sems = rest[n_in + n_out :]
    depth = ring.shape[0]
    slots = tiles.shape[0]
    unused = acc.shape[0] - 1
    first, end = begin[0], stop[0]
    steps = (end - first + CHUNK - 1) // CHUNK

    def place(step, j):
        return jnp.minimum(first + step * CHUNK + j, slots - 1)

    def fetch(step):
        at = lax.rem(step, depth)
        if not mirror:
            whole = tiles.at[pl.ds(step * CHUNK, CHUNK)]
            pltpu.make_async_copy(whole, ring.at[at], ring_sems.at[at]).start()
            return
        for j in range(CHUNK):
            tile = tiles.at[order[place(step, j)]]
            pltpu.make_async_copy(tile, ring.at[at, j], ring_sems.at[at]).start()

    part = held.shape[0] // n_in
    copies = [
        pltpu.make_async_copy(v_in[j], held.at[pl.ds(j * part, part)], in_sems.at[j])
        for j in range(n_in)
    ]
    for copy in copies:
        copy.start()
    for step in range(depth - 1):

        @pl.when(step < steps)
        def _():
            fetch(step)

    acc[...] = jnp.zeros_like(acc)
    for copy in copies:
        copy.wait()

    @pl.loop(0, steps)
    def _(step):
        @pl.when(step + depth - 1 < steps)
        def _():
            fetch(step + depth - 1)

        at = lax.rem(step, depth)
        pltpu.make_async_copy(tiles.at[pl.ds(0, CHUNK)], ring.at[at], ring_sems.at[at]).wait()
        for j in range(CHUNK):
            slot = place(step, j)
            out = jnp.where(first + step * CHUNK + j < end, out_slot[slot], unused)
            base = pl.multiple_of(in_slot[slot] * BS, BS)
            vec = held[pl.ds(base, BS), :]
            dims = (((0,), (0,)), ((), ())) if mirror else (((1,), (0,)), ((), ()))
            acc[out] += lax.dot_general(
                ring[at, j], vec, dims, preferred_element_type=jnp.float32
            )

    at = 0
    for out in outs:
        for b in range(out.shape[0] // BS):
            out[b * BS : (b + 1) * BS, :] = acc[at].astype(out.dtype)
            at += 1


def spmv(mirror, tiles, order, out_slot, in_slot, begin, stop, v_in, out_rows):
    slots = tiles.shape[0]
    n_in, n_out = len(v_in), len(out_rows)
    blocks_out = sum(out_rows) // BS
    return pl.pallas_call(
        functools.partial(spmv_kernel, mirror, n_in, n_out),
        in_specs=[pl.BlockSpec(memory_space=pltpu.SMEM)] * 5
        + [pl.BlockSpec(memory_space=pl.ANY)] * (1 + n_in),
        out_specs=[pl.BlockSpec(memory_space=pltpu.VMEM)] * n_out,
        scratch_shapes=[
            pltpu.VMEM((blocks_out + 1, BS, NV), jnp.float32),
            pltpu.VMEM((sum(v.shape[0] for v in v_in), NV), jnp.bfloat16),
            pltpu.VMEM((RING, CHUNK, BS, BS), jnp.bfloat16),
            pltpu.SemaphoreType.DMA((n_in,)),
            pltpu.SemaphoreType.DMA((RING,)),
        ],
        out_shape=[jax.ShapeDtypeStruct((n, NV), jnp.bfloat16) for n in out_rows],
        compiler_params=pltpu.CompilerParams(vmem_limit_bytes=LIMIT[mirror] * 2**20),
        cost_estimate=pl.CostEstimate(
            flops=2 * slots * BS * BS * NV, bytes_accessed=slots * BS * BS * 2, transcendentals=0
        ),
        name="mirror_sums" if mirror else "direct_sums",
    )(order, out_slot, in_slot, begin, stop, tiles, *v_in)


def gather_row(field):
    parts = {(0, 0): field, (0, 1): send_row(field, (0, 1))}
    for dx in (2, 1, 3):
        parts[dx, 0] = send_row(field, (dx, 0))
    for dx in (1, 3):
        parts[dx, 1] = send_row(parts[0, 1], (dx, 0))
    parts[2, 1] = send_row(parts[2, 0], (0, 1))
    return [parts[step] for step in ROW_STEPS]


def gather_col(field):
    return [lax.all_gather(field, "col", axis=0, tiled=True)]


def total(parts):
    return sum(part.astype(jnp.float32) for part in parts)


def rounded(parts):
    return parts[0] if len(parts) == 1 else total(parts).astype(jnp.bfloat16)


def scatter(send, own, beside, up, far, far_beside, down):
    rows = own[0].shape[0]
    passed = send(rounded(far_beside), (0, 1))
    up, down = send(rounded(up), (1, 0)), send(rounded(down), (3, 0))
    far = send(rounded(far + [passed]), (2, 0))
    beside = send(rounded(beside + [up[rows:], down[rows:]]), (0, 1))
    return own + [up[:rows], down[:rows], far, beside]


def apply(field, tiles, direct, mirror, first, rest):
    rows = OWN * BS
    split = [rows, rows, 2 * rows, rows, rows, 2 * rows]
    row_parts = gather_row(field)
    col_parts = gather_col(field)
    *mine, other = spmv(False, tiles, *direct, row_parts, split + [8 * rows])
    theirs = jnp.split(send_col(other, (0, 0), 1), [rows, 2 * rows, 4 * rows, 5 * rows, 6 * rows])
    early = spmv(True, tiles, *mirror, *first, col_parts, [2 * rows, 2 * rows, rows])
    rest, up, down, far_beside = lax.optimization_barrier((rest, *early))
    own, beside, far = spmv(True, tiles, *mirror, *rest, col_parts, [rows] * 3)
    parts = scatter(send_col, *([a, b] for a, b in zip(mine, theirs)))
    parts += scatter(send_row, [own], [beside], [up], [far], [far_beside], [down])
    return total(parts)


def local(vectors, tiles, tile_rows, tile_cols, tile_count):
    row_at = lax.axis_index("row")
    col_at = lax.axis_index("col")
    x, yh = row_at // 2, row_at % 2
    z, yl, k = col_at // 4, col_at // 2 % 2, col_at % 2
    live = jnp.arange(tiles.shape[0], dtype=jnp.int32) < tile_count[0]
    own_r = tile_rows // OWN
    oz, oy, ok = own_r // 4, own_r // 2 % 2, own_r % 2
    to_col = ((oz - z) % 4 * 2 + (oy ^ yl) + (ok ^ k) * 8) * OWN + tile_rows % OWN
    from_col = tile_rows
    own_c = tile_cols // OWN
    ox, oh = own_c // 2, own_c % 2
    dx = (ox - x) % 4
    dy = oh ^ yh
    to_row = jnp.where(dx % 2 == 1, dx // 2 * 2 + dy, jnp.where(dx == 0, dy, 2 + dy * 2))
    to_row = to_row * OWN + tile_cols % OWN
    from_row = ((x - ox) % 4 * 2 + (oh ^ yh)) * OWN + tile_cols % OWN
    at = jnp.arange(tiles.shape[0], dtype=jnp.int32)
    early = (dx % 2 == 1) | ((dx == 2) & (dy == 1))
    group = jnp.where(live, jnp.where(early, 0, 1), 2)
    ahead = (group[None, :] < group[:, None]) | (
        (group[None, :] == group[:, None]) & (at[None, :] < at[:, None])
    )
    place = jnp.sum(ahead.astype(jnp.int32), axis=1)
    chosen = place[None, :] == at[:, None]

    def ordered(values):
        return jnp.sum(jnp.where(chosen, values[None, :], 0), axis=1)

    early_count = jnp.sum((group == 0).astype(jnp.int32), keepdims=True)
    none = jnp.zeros((1,), jnp.int32)
    direct = (at, jnp.where(live, to_col, 0), jnp.where(live, from_row, 0), none, tile_count)
    mirror = (
        ordered(at),
        ordered(jnp.where(live, to_row, 0)),
        ordered(jnp.where(live, from_col, 0)),
    )
    direct, mirror, early_count = lax.optimization_barrier((direct, mirror, early_count))
    first, rest = (none, early_count), (early_count, tile_count)
    x_float = vectors.astype(jnp.float32)
    applied = apply(vectors, tiles, direct, mirror, first, rest)
    first_term = ((applied - center_value * x_float) / radius_value).astype(jnp.bfloat16)
    second = apply(first_term, tiles, direct, mirror, first, rest)
    return 2.0 * (second - center_value * first_term.astype(jnp.float32)) / radius_value - x_float


def solution(mesh):
    return jax.shard_map(
        local,
        mesh=mesh,
        in_specs=(
            P(("row", "col"), None),
            P(("row", "col"), None, None),
            P(("row", "col")),
            P(("row", "col")),
            P(("row", "col")),
        ),
        out_specs=P(("row", "col"), None),
        check_vma=False,
    )
```

```python
import functools

import jax
import jax.numpy as jnp
from jax import lax
from jax.experimental import pallas as pl
from jax.experimental.pallas import tpu as pltpu
from jax.sharding import PartitionSpec as P

center_value = 0.5
radius_value = 1.5

BS = 256
NV = 128
OWN = 4
CHUNK = 16
RING = 3
LIMIT = {False: 48, True: 60}

ROW_STEPS = [(dx, dy) for dx in range(4) for dy in range(2)]
COL_STEPS = [(dz, dy) for dz in range(4) for dy in range(2)]


def send_row(value, step):
    dx, dy = step
    pairs = [(x * 2 + y, (x + dx) % 4 * 2 + (y ^ dy)) for x in range(4) for y in range(2)]
    return lax.ppermute(value, "row", pairs)


def send_col(value, step, dk=0):
    dz, dy = step
    pairs = [
        (z * 4 + y * 2 + k, (z + dz) % 4 * 4 + (y ^ dy) * 2 + (k ^ dk))
        for z in range(4)
        for y in range(2)
        for k in range(2)
    ]
    return lax.ppermute(value, "col", pairs)


def spmv_kernel(mirror, n_in, n_out, order, out_slot, in_slot, bounds, tiles, *rest):
    v_in = rest[:n_in]
    outs = rest[n_in : n_in + n_out]
    acc, held, ring, in_sems, ring_sems = rest[n_in + n_out :]
    depth = ring.shape[0]
    slots = tiles.shape[0]
    unused = acc.shape[0] - 1
    first, end = bounds[0], bounds[1]
    steps = (end - first + CHUNK - 1) // CHUNK

    def place(step, j):
        return jnp.minimum(first + step * CHUNK + j, slots - 1)

    def fetch(step):
        at = lax.rem(step, depth)
        if not mirror:
            whole = tiles.at[pl.ds(step * CHUNK, CHUNK)]
            pltpu.make_async_copy(whole, ring.at[at], ring_sems.at[at]).start()
            return
        for j in range(CHUNK):
            tile = tiles.at[order[place(step, j)]]
            pltpu.make_async_copy(tile, ring.at[at, j], ring_sems.at[at]).start()

    part = held.shape[0] // n_in
    copies = [
        pltpu.make_async_copy(v_in[j], held.at[pl.ds(j * part, part)], in_sems.at[j])
        for j in range(n_in)
    ]
    for copy in copies:
        copy.start()
    for step in range(depth - 1):

        @pl.when(step < steps)
        def _():
            fetch(step)

    acc[...] = jnp.zeros_like(acc)
    for copy in copies:
        copy.wait()

    @pl.loop(0, steps)
    def _(step):
        @pl.when(step + depth - 1 < steps)
        def _():
            fetch(step + depth - 1)

        at = lax.rem(step, depth)
        pltpu.make_async_copy(tiles.at[pl.ds(0, CHUNK)], ring.at[at], ring_sems.at[at]).wait()
        for j in range(CHUNK):
            slot = place(step, j)
            out = jnp.where(first + step * CHUNK + j < end, out_slot[slot], unused)
            base = pl.multiple_of(in_slot[slot] * BS, BS)
            vec = held[pl.ds(base, BS), :]
            dims = (((0,), (0,)), ((), ())) if mirror else (((1,), (0,)), ((), ()))
            acc[out] += lax.dot_general(
                ring[at, j], vec, dims, preferred_element_type=jnp.float32
            )

    at = 0
    for out in outs:
        for b in range(out.shape[0] // BS):
            out[b * BS : (b + 1) * BS, :] = acc[at].astype(out.dtype)
            at += 1


def spmv(mirror, tiles, order, out_slot, in_slot, bounds, v_in, out_rows):
    slots = tiles.shape[0]
    n_in, n_out = len(v_in), len(out_rows)
    blocks_out = sum(out_rows) // BS
    return pl.pallas_call(
        functools.partial(spmv_kernel, mirror, n_in, n_out),
        in_specs=[pl.BlockSpec(memory_space=pltpu.SMEM)] * 4
        + [pl.BlockSpec(memory_space=pl.ANY)] * (1 + n_in),
        out_specs=[pl.BlockSpec(memory_space=pltpu.VMEM)] * n_out,
        scratch_shapes=[
            pltpu.VMEM((blocks_out + 1, BS, NV), jnp.float32),
            pltpu.VMEM((sum(v.shape[0] for v in v_in), NV), jnp.bfloat16),
            pltpu.VMEM((RING, CHUNK, BS, BS), jnp.bfloat16),
            pltpu.SemaphoreType.DMA((n_in,)),
            pltpu.SemaphoreType.DMA((RING,)),
        ],
        out_shape=[jax.ShapeDtypeStruct((n, NV), jnp.bfloat16) for n in out_rows],
        compiler_params=pltpu.CompilerParams(vmem_limit_bytes=LIMIT[mirror] * 2**20),
        cost_estimate=pl.CostEstimate(
            flops=2 * slots * BS * BS * NV, bytes_accessed=slots * BS * BS * 2, transcendentals=0
        ),
        name="mirror_sums" if mirror else "direct_sums",
    )(order, out_slot, in_slot, bounds, tiles, *v_in)


def gather_row(field):
    parts = {(0, 0): field, (0, 1): send_row(field, (0, 1))}
    for dx in (2, 1, 3):
        parts[dx, 0] = send_row(field, (dx, 0))
    for dx in (1, 3):
        parts[dx, 1] = send_row(parts[0, 1], (dx, 0))
    parts[2, 1] = send_row(parts[2, 0], (0, 1))
    return [parts[step] for step in ROW_STEPS]


def gather_col(field):
    return [lax.all_gather(field, "col", axis=0, tiled=True)]


def total(parts):
    return sum(part.astype(jnp.float32) for part in parts)


def rounded(parts):
    return parts[0] if len(parts) == 1 else total(parts).astype(jnp.bfloat16)


def scatter(send, own, beside, up, far, far_beside, down):
    rows = own[0].shape[0]
    passed = send(rounded(far_beside), (0, 1))
    up, down = send(rounded(up), (1, 0)), send(rounded(down), (3, 0))
    far = send(rounded(far + [passed]), (2, 0))
    beside = send(rounded(beside + [up[rows:], down[rows:]]), (0, 1))
    return own + [up[:rows], down[:rows], far, beside]


def apply(field, tiles, direct, mirror, first, rest):
    rows = OWN * BS
    split = [rows, rows, 2 * rows, rows, rows, 2 * rows]
    row_parts = gather_row(field)
    col_parts = gather_col(field)
    *mine, other = spmv(False, tiles, *direct, row_parts, split + [8 * rows])
    theirs = jnp.split(send_col(other, (0, 0), 1), [rows, 2 * rows, 4 * rows, 5 * rows, 6 * rows])
    early = spmv(True, tiles, *mirror, first, col_parts, [2 * rows, 2 * rows, rows])
    rest, up, down, far_beside = lax.optimization_barrier((rest, *early))
    own, beside, far = spmv(True, tiles, *mirror, rest, col_parts, [rows] * 3)
    parts = scatter(send_col, *([a, b] for a, b in zip(mine, theirs)))
    parts += scatter(send_row, [own], [beside], [up], [far], [far_beside], [down])
    return total(parts)


def local(vectors, tiles, tile_rows, tile_cols, tile_count):
    row_at = lax.axis_index("row")
    col_at = lax.axis_index("col")
    x, yh = row_at // 2, row_at % 2
    z, yl, k = col_at // 4, col_at // 2 % 2, col_at % 2
    live = jnp.arange(tiles.shape[0], dtype=jnp.int32) < tile_count[0]
    own_r = tile_rows // OWN
    oz, oy, ok = own_r // 4, own_r // 2 % 2, own_r % 2
    to_col = ((oz - z) % 4 * 2 + (oy ^ yl) + (ok ^ k) * 8) * OWN + tile_rows % OWN
    from_col = tile_rows
    own_c = tile_cols // OWN
    ox, oh = own_c // 2, own_c % 2
    dx = (ox - x) % 4
    dy = oh ^ yh
    to_row = jnp.where(dx % 2 == 1, dx // 2 * 2 + dy, jnp.where(dx == 0, dy, 2 + dy * 2))
    to_row = to_row * OWN + tile_cols % OWN
    from_row = ((x - ox) % 4 * 2 + (oh ^ yh)) * OWN + tile_cols % OWN
    at = jnp.arange(tiles.shape[0], dtype=jnp.int32)
    early = (dx % 2 == 1) | ((dx == 2) & (dy == 1))
    group = jnp.where(live, jnp.where(early, 0, 1), 2)
    ahead = (group[None, :] < group[:, None]) | (
        (group[None, :] == group[:, None]) & (at[None, :] < at[:, None])
    )
    place = jnp.sum(ahead.astype(jnp.int32), axis=1)
    chosen = place[None, :] == at[:, None]

    def ordered(values):
        return jnp.sum(jnp.where(chosen, values[None, :], 0), axis=1)

    live_count = tile_count[0]
    early_count = jnp.sum((group == 0).astype(jnp.int32))
    zero = jnp.zeros((), jnp.int32)
    whole = jnp.stack([zero, live_count])
    first = jnp.stack([zero, early_count])
    rest = jnp.stack([early_count, live_count])
    direct = (at, jnp.where(live, to_col, 0), jnp.where(live, from_row, 0), whole)
    mirror = (
        ordered(at),
        ordered(jnp.where(live, to_row, 0)),
        ordered(jnp.where(live, from_col, 0)),
    )
    x_float = vectors.astype(jnp.float32)
    applied = apply(vectors, tiles, direct, mirror, first, rest)
    first_term = ((applied - center_value * x_float) / radius_value).astype(jnp.bfloat16)
    second = apply(first_term, tiles, direct, mirror, first, rest)
    return 2.0 * (second - center_value * first_term.astype(jnp.float32)) / radius_value - x_float


def solution(mesh):
    return jax.shard_map(
        local,
        mesh=mesh,
        in_specs=(
            P(("row", "col"), None),
            P(("row", "col"), None, None),
            P(("row", "col")),
            P(("row", "col")),
            P(("row", "col")),
        ),
        out_specs=P(("row", "col"), None),
        check_vma=False,
    )
```

```python
import functools

import jax
import jax.numpy as jnp
from jax import lax
from jax.experimental import pallas as pl
from jax.experimental.pallas import tpu as pltpu
from jax.sharding import PartitionSpec as P

center_value = 0.5
radius_value = 1.5

BS = 256
NV = 128
OWN = 4
CHUNK = 16
RING = 4
LIMIT = {False: 48, True: 60}

ROW_STEPS = [(dx, dy) for dx in range(4) for dy in range(2)]
COL_STEPS = [(dz, dy) for dz in range(4) for dy in range(2)]


def send_row(value, step):
    dx, dy = step
    pairs = [(x * 2 + y, (x + dx) % 4 * 2 + (y ^ dy)) for x in range(4) for y in range(2)]
    return lax.ppermute(value, "row", pairs)


def send_col(value, step, dk=0):
    dz, dy = step
    pairs = [
        (z * 4 + y * 2 + k, (z + dz) % 4 * 4 + (y ^ dy) * 2 + (k ^ dk))
        for z in range(4)
        for y in range(2)
        for k in range(2)
    ]
    return lax.ppermute(value, "col", pairs)


def spmv_kernel(mirror, n_in, n_out, out_slot, in_slot, count, tiles, *rest):
    v_in = rest[:n_in]
    outs = rest[n_in : n_in + n_out]
    acc, held, ring, in_sems, ring_sems = rest[n_in + n_out :]
    depth = ring.shape[0]
    steps = (count[0] + CHUNK - 1) // CHUNK

    def fetch(step):
        at = lax.rem(step, depth)
        return pltpu.make_async_copy(
            tiles.at[pl.ds(step * CHUNK, CHUNK)], ring.at[at], ring_sems.at[at]
        )

    part = held.shape[0] // n_in
    copies = [
        pltpu.make_async_copy(v_in[j], held.at[pl.ds(j * part, part)], in_sems.at[j])
        for j in range(n_in)
    ]
    for copy in copies:
        copy.start()
    for step in range(depth - 1):

        @pl.when(step < steps)
        def _():
            fetch(step).start()

    acc[...] = jnp.zeros_like(acc)
    for copy in copies:
        copy.wait()

    @pl.loop(0, steps)
    def _(step):
        @pl.when(step + depth - 1 < steps)
        def _():
            fetch(step + depth - 1).start()

        fetch(step).wait()
        at = lax.rem(step, depth)
        for j in range(CHUNK):
            slot = step * CHUNK + j
            base = pl.multiple_of(in_slot[slot] * BS, BS)
            vec = held[pl.ds(base, BS), :]
            dims = (((0,), (0,)), ((), ())) if mirror else (((1,), (0,)), ((), ()))
            acc[out_slot[slot]] += lax.dot_general(
                ring[at, j], vec, dims, preferred_element_type=jnp.float32
            )

    at = 0
    for out in outs:
        for b in range(out.shape[0] // BS):
            out[b * BS : (b + 1) * BS, :] = acc[at].astype(out.dtype)
            at += 1


def spmv(mirror, tiles, out_slot, in_slot, count, v_in, out_rows):
    slots = tiles.shape[0]
    n_in, n_out = len(v_in), len(out_rows)
    blocks_out = sum(out_rows) // BS
    return pl.pallas_call(
        functools.partial(spmv_kernel, mirror, n_in, n_out),
        in_specs=[pl.BlockSpec(memory_space=pltpu.SMEM)] * 3
        + [pl.BlockSpec(memory_space=pl.ANY)] * (1 + n_in),
        out_specs=[pl.BlockSpec(memory_space=pltpu.VMEM)] * n_out,
        scratch_shapes=[
            pltpu.VMEM((blocks_out + 1, BS, NV), jnp.float32),
            pltpu.VMEM((sum(v.shape[0] for v in v_in), NV), jnp.bfloat16),
            pltpu.VMEM((RING, CHUNK, BS, BS), jnp.bfloat16),
            pltpu.SemaphoreType.DMA((n_in,)),
            pltpu.SemaphoreType.DMA((RING,)),
        ],
        out_shape=[jax.ShapeDtypeStruct((n, NV), jnp.bfloat16) for n in out_rows],
        compiler_params=pltpu.CompilerParams(vmem_limit_bytes=LIMIT[mirror] * 2**20),
        cost_estimate=pl.CostEstimate(
            flops=2 * slots * BS * BS * NV, bytes_accessed=slots * BS * BS * 2, transcendentals=0
        ),
        name="mirror_sums" if mirror else "direct_sums",
    )(out_slot, in_slot, count, tiles, *v_in)


def gather_row(field):
    parts = {(0, 0): field, (0, 1): send_row(field, (0, 1))}
    for dx in (2, 1, 3):
        parts[dx, 0] = send_row(field, (dx, 0))
    for dx in (1, 3):
        parts[dx, 1] = send_row(parts[0, 1], (dx, 0))
    parts[2, 1] = send_row(parts[2, 0], (0, 1))
    return [parts[step] for step in ROW_STEPS]


def gather_col(field):
    return [lax.all_gather(field, "col", axis=0, tiled=True)]


def total(parts):
    return sum(part.astype(jnp.float32) for part in parts)


def rounded(parts):
    return parts[0] if len(parts) == 1 else total(parts).astype(jnp.bfloat16)


def scatter(send, own, beside, up, far, far_beside, down):
    rows = own[0].shape[0]
    passed = send(rounded(far_beside), (0, 1))
    up, down = send(rounded(up), (1, 0)), send(rounded(down), (3, 0))
    far = send(rounded(far + [passed]), (2, 0))
    beside = send(rounded(beside + [up[rows:], down[rows:]]), (0, 1))
    return own + [up[:rows], down[:rows], far, beside]


def apply(field, tiles, slots, count):
    direct_out, direct_in, mirror_out, mirror_in = slots
    rows = OWN * BS
    split = [rows, rows, 2 * rows, rows, rows, 2 * rows]
    row_parts = gather_row(field)
    col_parts = gather_col(field)
    *mine, other = spmv(False, tiles, direct_out, direct_in, count, row_parts, split + [8 * rows])
    theirs = jnp.split(send_col(other, (0, 0), 1), [rows, 2 * rows, 4 * rows, 5 * rows, 6 * rows])
    mirrored = spmv(True, tiles, mirror_out, mirror_in, count, col_parts, split)
    parts = scatter(send_col, *([a, b] for a, b in zip(mine, theirs)))
    parts += scatter(send_row, *([a] for a in mirrored))
    return total(parts)


def local(vectors, tiles, tile_rows, tile_cols, tile_count):
    row_at = lax.axis_index("row")
    col_at = lax.axis_index("col")
    x, yh = row_at // 2, row_at % 2
    z, yl, k = col_at // 4, col_at // 2 % 2, col_at % 2
    live = jnp.arange(tiles.shape[0], dtype=jnp.int32) < tile_count[0]
    own_r = tile_rows // OWN
    oz, oy, ok = own_r // 4, own_r // 2 % 2, own_r % 2
    to_col = ((oz - z) % 4 * 2 + (oy ^ yl) + (ok ^ k) * 8) * OWN + tile_rows % OWN
    from_col = tile_rows
    own_c = tile_cols // OWN
    ox, oh = own_c // 2, own_c % 2
    to_row = ((ox - x) % 4 * 2 + (oh ^ yh)) * OWN + tile_cols % OWN
    from_row = ((x - ox) % 4 * 2 + (oh ^ yh)) * OWN + tile_cols % OWN
    slots = (
        jnp.where(live, to_col, 16 * OWN),
        jnp.where(live, from_row, 0),
        jnp.where(live, to_row, 8 * OWN),
        jnp.where(live, from_col, 0),
    )
    x_float = vectors.astype(jnp.float32)
    applied = apply(vectors, tiles, slots, tile_count)
    first_term = ((applied - center_value * x_float) / radius_value).astype(jnp.bfloat16)
    second = apply(first_term, tiles, slots, tile_count)
    return 2.0 * (second - center_value * first_term.astype(jnp.float32)) / radius_value - x_float


def solution(mesh):
    return jax.shard_map(
        local,
        mesh=mesh,
        in_specs=(
            P(("row", "col"), None),
            P(("row", "col"), None, None),
            P(("row", "col")),
            P(("row", "col")),
            P(("row", "col")),
        ),
        out_specs=P(("row", "col"), None),
        check_vma=False,
    )
```
